128 devices in a mesh: row: 8 (over z, core), col: 16 (over y, x).
Axes of the slice: x: 4, y: 4, z: 4, core: 2. Of those that a mesh axis runs over, the one named last changes fastest.
Arguments:
- state_cells: float32 [5, 32768, 1024], P(None, ('row', 'col')), may hold values from -1 to 6, as said below
- target: int32 [1024], P(('row', 'col')), may hold values from 0 to 1023, as said below
Outputs:
- advanced: float32 [5, 32768, 1024], P(None, ('row', 'col'))
The draws below stay inside these ranges and needn't reach their ends.
Inputs may be any that keep to these rules, and one draw needn't show every extreme that they name: target is a permutation of all box indices. A box held by the device in row r and col c goes to the device in row r whose col index is c + 1, c, c - 1 or the one half the col axis away from c (cyclically over the col axis), and each device sends exactly a quarter of its 8 boxes to each of these four devices. `state_cells`: density and pressure lie between 1 and 2 and each velocity component between -0.5 and 0.5 in every cell; the last field is the total energy for a ratio of specific heats of 1.4.
All inputs are finite; a program needn't handle non-finite values.
Results may differ from the reference program's by a relative error of at most 0.00002.
Values sent between devices are 32-bit elements; how exact they have to be, the bound alone decides.
No kernel may reach another device: no remote copies, remote signals or barrier semaphores. Data moves between devices by JAX's collectives and lax.ppermute only.
A program may use at most 128 MiB of HBM per device.

```python
import jax
import jax.numpy as jnp
from jax import lax

BOX_EDGE = 32
BOX_DEV = 8
BOXES = 1024
N_ROW = 8
N_COL = 16


def draw_state_cells(key, part):
    key = jax.random.fold_in(key, 5)
    density_key, xvel_key, yvel_key, zvel_key, pressure_key = jax.random.split(key, 5)
    shape = (BOXES * BOX_EDGE, BOX_EDGE * BOX_EDGE)
    density = jax.random.uniform(density_key, shape, jnp.float32, 1.0, 2.0)
    xvelocity = jax.random.uniform(xvel_key, shape, jnp.float32, -0.5, 0.5)
    yvelocity = jax.random.uniform(yvel_key, shape, jnp.float32, -0.5, 0.5)
    zvelocity = jax.random.uniform(zvel_key, shape, jnp.float32, -0.5, 0.5)
    pressure = jax.random.uniform(pressure_key, shape, jnp.float32, 1.0, 2.0)
    energy = pressure / 0.4 + 0.5 * density * (xvelocity * xvelocity + yvelocity * yvelocity + zvelocity * zvelocity)
    return jnp.stack([density, density * xvelocity, density * yvelocity, density * zvelocity, energy]).astype(jnp.float32)


def draw_target(key, part):
    key = jax.random.fold_in(key, 11)
    group_key, slot_key = jax.random.split(key)
    per_peer = BOX_DEV // 4
    offsets = jnp.array([0, -1, 1, N_COL // 2], dtype=jnp.int32)
    four_index = jnp.arange(4, dtype=jnp.int32)
    group_scores = jax.random.randint(group_key, (N_ROW, N_COL, 4), 0, 1 << 20) * 4 + four_index
    group_perm = jnp.argsort(group_scores, axis=-1).astype(jnp.int32)
    group_pos = jnp.argsort(group_perm, axis=-1).astype(jnp.int32)
    slot_index = jnp.arange(BOX_DEV, dtype=jnp.int32)
    slot_scores = jax.random.randint(slot_key, (N_ROW, N_COL, BOX_DEV), 0, 1 << 20) * BOX_DEV + slot_index
    slot_perm = jnp.argsort(slot_scores, axis=-1).astype(jnp.int32)
    col_index = jnp.arange(N_COL, dtype=jnp.int32)[:, None]
    dest_col = (col_index - offsets[None, :]) % N_COL
    dest_group = group_pos[:, dest_col, four_index[None, :]]
    row_index = jnp.arange(N_ROW, dtype=jnp.int32)[:, None, None]
    base_id = (row_index * N_COL + dest_col[None, :, :]) * BOX_DEV + dest_group * per_peer
    new_ids = base_id[..., None] + jnp.arange(per_peer, dtype=jnp.int32)
    new_flat = new_ids.reshape(N_ROW, N_COL, BOX_DEV)
    inverse = jnp.argsort(slot_perm, axis=-1).astype(jnp.int32)
    target = jnp.take_along_axis(new_flat, inverse, axis=-1)
    return target.reshape(BOXES).astype(jnp.int32)


def setup_inputs(seed: int = 0) -> dict:
    key_list = jax.random.split(jax.random.key(seed), 3)
    return {
        "state_cells": draw_state_cells(jax.random.fold_in(key_list[2], 71), 0),
        "target": draw_target(jax.random.fold_in(key_list[2], 71), 0),
    }


gamma_ratio = 1.4
time_ratio = 0.05
weno_eps = 1e-06

def square(value):
    return value * value

def reconstruct(value_a, value_b, value_c, value_d, value_e):
    guess_zero = (2.0 * value_a - 7.0 * value_b + 11.0 * value_c) / 6.0
    guess_one = (-value_b + 5.0 * value_c + 2.0 * value_d) / 6.0
    guess_two = (2.0 * value_c + 5.0 * value_d - value_e) / 6.0
    rough_zero = 13.0 / 12.0 * square(value_a - 2.0 * value_b + value_c) + 0.25 * square(value_a - 4.0 * value_b + 3.0 * value_c)
    rough_one = 13.0 / 12.0 * square(value_b - 2.0 * value_c + value_d) + 0.25 * square(value_b - value_d)
    rough_two = 13.0 / 12.0 * square(value_c - 2.0 * value_d + value_e) + 0.25 * square(3.0 * value_c - 4.0 * value_d + value_e)
    weight_zero = 0.1 / square(weno_eps + rough_zero)
    weight_one = 0.6 / square(weno_eps + rough_one)
    weight_two = 0.3 / square(weno_eps + rough_two)
    weight_sum = weight_zero + weight_one + weight_two
    return (weight_zero * guess_zero + weight_one * guess_one + weight_two * guess_two) / weight_sum

def physics(padded):
    density = padded[0]
    xmomentum = padded[1]
    ymomentum = padded[2]
    zmomentum = padded[3]
    energy = padded[4]
    velocity = xmomentum / density
    kinetic = 0.5 * (xmomentum * xmomentum + ymomentum * ymomentum + zmomentum * zmomentum) / density
    pressure = (gamma_ratio - 1.0) * (energy - kinetic)
    fluxes = (xmomentum, xmomentum * velocity + pressure, ymomentum * velocity, zmomentum * velocity, (energy + pressure) * velocity)
    speeds = jnp.abs(velocity) + jnp.sqrt(gamma_ratio * pressure / density)
    return (fluxes, speeds)

def increment(padded):
    fluxes, speeds = physics(padded)
    face_count = padded.shape[1] - 5
    dissipation = jnp.maximum(speeds[2:2 + face_count], speeds[3:3 + face_count])
    changes = []
    for component in range(5):
        field_flux = fluxes[component]
        conserved = padded[component]
        forward = [0.5 * (field_flux[offset:offset + face_count] + dissipation * conserved[offset:offset + face_count]) for offset in range(6)]
        backward = [0.5 * (field_flux[offset:offset + face_count] - dissipation * conserved[offset:offset + face_count]) for offset in range(6)]
        face_flux = reconstruct(forward[0], forward[1], forward[2], forward[3], forward[4]) + reconstruct(backward[5], backward[4], backward[3], backward[2], backward[1])
        changes.append(-time_ratio * (face_flux[1:] - face_flux[:-1]))
    return jnp.stack(changes)

def wrap_pad(whole_line):
    return jnp.concatenate([whole_line[:, -3:], whole_line, whole_line[:, :3]], axis=1)

def advance(whole_line):
    section_one = whole_line + increment(wrap_pad(whole_line))
    return 0.5 * whole_line + 0.5 * (section_one + increment(wrap_pad(section_one)))

def reference(state_cells, target):
    box_data = state_cells.reshape(5, BOXES, BOX_EDGE, BOX_EDGE * BOX_EDGE)
    moved = jnp.zeros_like(box_data).at[:, target].set(box_data)
    whole_line = moved.reshape(5, BOXES * BOX_EDGE, BOX_EDGE * BOX_EDGE)
    blocks = whole_line.reshape(5, BOXES * BOX_EDGE, BOX_EDGE * BOX_EDGE // 64, 64).transpose(2, 0, 1, 3)
    advanced = lax.map(advance, blocks)
    return advanced.transpose(1, 2, 0, 3).reshape(5, BOXES * BOX_EDGE, BOX_EDGE * BOX_EDGE)
```

```python
import functools

import jax
import jax.numpy as jnp
from jax import lax
from jax.experimental import pallas as pl
from jax.experimental.pallas import tpu as pltpu
from jax.sharding import PartitionSpec as P

FIELDS = 5
EDGE = 32
SLOTS = 8
LANES = 128
TILES = 8
CHUNKS = (4, 3, 1)
PIECES = ((4, 4), (4, 4), (4, 3, 1))
OFFSETS = (0, 1, -1, 8)
STEP = 0.05 / 6.0
ANY = pl.BlockSpec(memory_space=pltpu.HBM)
SMEM = pl.BlockSpec(memory_space=pltpu.SMEM)
F32 = jnp.float32


def params():
    return pltpu.CompilerParams(vmem_limit_bytes=60 << 20)


def side(t0, t1, t2, a01, a12):
    u0, u1, u2 = t0 * t0, t1 * t1, t2 * t2
    v = 3.0 * u0
    w = u2 + u2
    return (u1 * (w * a01 + v * a12)) * pl.reciprocal(u1 * (u2 + v) + v * w, approx=True)


def rough(first):
    return (13.0 / 3.0 * first) * first + 0.75e-6


def square(value):
    return value * value


def face_value(au, ag, fu, fg, base, beta):
    bu = [beta * value for value in au]
    ap = [ag[i] + bu[i] for i in range(3)]
    am = [ag[i] - bu[i] for i in range(1, 4)]
    bf = [beta * value for value in fu]
    fp1, fp2 = fg[0] + bf[0], fg[1] + bf[1]
    fm1, fm2 = fg[2] - bf[2], fg[1] - bf[1]
    x1, x2 = rough(fp1), rough(fp2)
    plus = side(
        square(ap[0] + fp1) + x1, square(ap[1] + fp1) + x1, square(ap[2] - fp2) + x2, ap[0] - ap[1], ap[1] - ap[2]
    )
    x1, x2 = rough(fm1), rough(fm2)
    minus = side(
        square(am[2] - fm1) + x1, square(am[1] - fm1) + x1, square(am[0] + fm2) + x2, am[2] - am[1], am[1] - am[0]
    )
    return (base - (bu[1] - bu[2])) + (plus + minus)


def physics(count, us, gs, bs):
    previous = None
    for i in range(count):
        u = [us[f, i] for f in range(FIELDS)]
        r = 1.0 / u[0]
        half_velocity = (0.5 * u[1]) * r
        kinetic = (0.5 * r) * (u[1] * u[1] + u[2] * u[2] + u[3] * u[3])
        half_pressure = 0.2 * (u[4] - kinetic)
        gs[0, i] = 0.5 * u[1]
        gs[1, i] = u[1] * half_velocity + half_pressure
        gs[2, i] = u[2] * half_velocity
        gs[3, i] = u[3] * half_velocity
        gs[4, i] = (u[4] + (half_pressure + half_pressure)) * half_velocity
        speed = jnp.abs(half_velocity) + jnp.sqrt((0.7 * half_pressure) * r)
        if previous is not None:
            bs[i - 1] = jnp.maximum(previous, speed)
        previous = speed


def update(count, us, gs, bs, f, emit):
    u, g, fu, fg, au, ag, su, sg, base = ({} for _ in range(9))

    def cell(i):
        u[i], g[i] = us[f, i], gs[f, i]
        if i:
            fu[i], fg[i] = u[i] - u[i - 1], g[i] - g[i - 1]
        if i >= 2:
            su[i], sg[i] = 0.375 * fu[i], 0.375 * fg[i]
            au[i - 1], ag[i - 1] = fu[i] - fu[i - 1], fg[i] - fg[i - 1]
            base[i - 1] = 6.0 * g[i - 1] - ag[i - 1]

    for i in range(5):
        cell(i)
    previous = None
    for i in range(2, count + 3):
        cell(i + 3)
        face = face_value(
            [au[j] for j in range(i - 1, i + 3)],
            [ag[j] for j in range(i - 1, i + 3)],
            [su[j] for j in range(i, i + 3)],
            [sg[j] for j in range(i, i + 3)],
            base[i] + base[i + 1],
            bs[i],
        )
        if previous is not None:
            emit(i - 3, u[i], face - previous)
        previous = face


def ghosts(ref, f):
    for k in range(3):
        ref[f, k] = pltpu.roll(ref[f, EDGE + k], 1, 0)
        ref[f, EDGE + 3 + k] = pltpu.roll(ref[f, 3 + k], SLOTS - 1, 0)


def pack_kernel(pieces, first, target, state, *refs):
    count = len(pieces)
    outs, (stage, notes, in_sem, out_sem, note_sem) = refs[:count], refs[count:]
    col = lax.axis_index("col")
    steps = [((target[box] // SLOTS) - col) & 15 for box in range(SLOTS)]
    places, slots = [], []
    for peer in range(3):
        seen, place, slot = jnp.int32(0), [jnp.int32(0)] * 2, [jnp.int32(0)] * 2
        for box in range(SLOTS):
            hit = steps[box] == (OFFSETS[peer + 1] & 15)
            for rank in range(2):
                mine = hit & (seen == rank)
                place[rank] = jnp.where(mine, box, place[rank])
                slot[rank] = jnp.where(mine, target[box] & 7, slot[rank])
            seen = seen + hit.astype(jnp.int32)
        places.append(place)
        slots.append(slot)

    low = min(start for _, start, _ in pieces) * LANES
    for i, (peer, start, tiles) in enumerate(pieces):
        columns = pl.ds(start * LANES, tiles * LANES)
        for rank in range(2):
            row = pl.multiple_of(places[peer][rank] * EDGE, EDGE)
            for f in range(FIELDS):
                pltpu.make_async_copy(
                    state.at[f, pl.ds(row, EDGE), columns],
                    stage.at[peer, pl.ds((rank * FIELDS + f) * EDGE, EDGE), pl.ds(start * LANES - low, tiles * LANES)],
                    in_sem.at[i],
                ).start()

    def note(peer, i):
        return pltpu.make_async_copy(
            notes.at[peer], outs[i].at[pl.ds(2 * FIELDS * EDGE, 8), pl.ds(0, LANES)], note_sem.at[peer]
        )

    def leave(i, peer, start, tiles):
        part = stage.at[peer, :, pl.ds(start * LANES - low, tiles * LANES)]
        return part, pltpu.make_async_copy(part, outs[i].at[pl.ds(0, 2 * FIELDS * EDGE), :], out_sem.at[i])

    if first:
        rows = lax.broadcasted_iota(jnp.int32, (8, LANES), 0)
        for i, (peer, _, _) in enumerate(pieces):
            notes[peer] = jnp.where(rows == 0, slots[peer][0], slots[peer][1]).astype(F32)
            note(peer, i).start()
    copies = []
    for i, piece in enumerate(pieces):
        part, copy = leave(i, *piece)
        pltpu.make_async_copy(part, part, in_sem.at[i]).wait()
        copy.start()
        copies.append(copy)
    for i, piece in enumerate(pieces):
        copies[i].wait()
        if first:
            note(piece[0], i).wait()


def pack(target, state, pieces, first):
    rows = 2 * FIELDS * EDGE
    low = min(start for _, start, _ in pieces)
    high = max(start + tiles for _, start, tiles in pieces)
    return pl.pallas_call(
        functools.partial(pack_kernel, pieces, first),
        in_specs=[SMEM, ANY],
        out_specs=[ANY] * len(pieces),
        out_shape=[jax.ShapeDtypeStruct((rows + 8 * first, tiles * LANES), F32) for _, _, tiles in pieces],
        scratch_shapes=[
            pltpu.VMEM((3, rows, (high - low) * LANES), F32),
            pltpu.VMEM((3, 8, LANES), F32),
            pltpu.SemaphoreType.DMA((len(pieces),)),
            pltpu.SemaphoreType.DMA((len(pieces),)),
            pltpu.SemaphoreType.DMA((3,)),
        ],
        compiler_params=params(),
        name="pack",
    )(target, state)


def table_kernel(target, one, two, three, table, notes, sem):
    def note(peer, ref):
        return pltpu.make_async_copy(
            ref.at[pl.ds(2 * FIELDS * EDGE, 8), pl.ds(0, LANES)], notes.at[peer], sem.at[peer]
        )

    for peer, ref in enumerate((one, two, three)):
        note(peer, ref).start()
    col = lax.axis_index("col")
    for box in range(SLOTS):

        @pl.when(((target[box] // SLOTS) & 15) == col)
        def _(box=box):
            table[target[box] & 7] = box

    for peer, ref in enumerate((one, two, three)):
        note(peer, ref).wait()
        for rank in range(2):
            table[notes[peer, rank, 0].astype(jnp.int32) & 7] = 8 * (peer + 1) + rank


def make_table(target, arrived):
    return pl.pallas_call(
        table_kernel,
        in_specs=[SMEM] + [ANY] * 3,
        out_specs=SMEM,
        out_shape=jax.ShapeDtypeStruct((SLOTS,), jnp.int32),
        scratch_shapes=[pltpu.SMEM((3, 8, LANES), F32), pltpu.SemaphoreType.DMA((3,))],
        compiler_params=params(),
        name="slots",
    )(target, *arrived)


def chunk_kernel(start, tiles, offsets, table, state, one, two, three, *refs):
    out, boxes, result, us, gs, bs, s1, in_sem, out_sem = refs[-9:]
    buffers = (None, one, two, three)

    box_rows = FIELDS * EDGE
    for tile in range(tiles):
        for slot in range(SLOTS):
            code = table[slot]

            @pl.when(code < SLOTS)
            def _(tile=tile, slot=slot, code=code):
                for f in range(FIELDS):
                    pltpu.make_async_copy(
                        state.at[f, pl.ds(pl.multiple_of(code * EDGE, EDGE), EDGE), pl.ds(start + tile * LANES, LANES)],
                        boxes.at[tile, pl.ds(slot * box_rows + f * EDGE, EDGE), :],
                        in_sem.at[tile],
                    ).start()

            for peer in range(1, 4):

                @pl.when((code >> 3) == peer)
                def _(tile=tile, slot=slot, code=code, peer=peer):
                    pltpu.make_async_copy(
                        buffers[peer].at[
                            pl.ds(pl.multiple_of((code & 7) * box_rows, EDGE), box_rows),
                            pl.ds((offsets[peer - 1] + tile) * LANES, LANES),
                        ],
                        boxes.at[tile, pl.ds(slot * box_rows, box_rows), :],
                        in_sem.at[tile],
                    ).start()

    def leave(tile, half):
        column = pl.multiple_of(start + tile * LANES, LANES)
        return pltpu.make_async_copy(result.at[half], out.at[:, :, pl.ds(column, LANES)], out_sem.at[half])

    @pl.loop(0, tiles)
    def _(tile):
        half = tile & 1
        pltpu.make_async_copy(boxes.at[tile], boxes.at[tile], in_sem.at[tile]).wait()

        @pl.loop(0, FIELDS)
        def _(f):
            for x in range(EDGE):
                us[f, 3 + x] = boxes[tile, pl.ds(f * EDGE + x, SLOTS, stride=box_rows), :]
            ghosts(us, f)

        physics(EDGE + 6, us, gs, bs)

        @pl.loop(0, FIELDS)
        def _(f):
            def emit(k, u, change):
                s1[f, 3 + k] = u - STEP * change

            update(EDGE, us, gs, bs, f, emit)
            ghosts(s1, f)

        physics(EDGE + 6, s1, gs, bs)

        @pl.when(tile >= 2)
        def _():
            leave(tile - 2, half).wait()

        @pl.loop(0, FIELDS)
        def _(f):
            def emit(k, u, change):
                result[half, f, pl.ds(k, SLOTS, stride=EDGE), :] = 0.5 * us[f, 3 + k] + (
                    0.5 * u - (0.5 * STEP) * change
                )

            update(EDGE, s1, gs, bs, f, emit)

        leave(tile, half).start()

    for tile in range(max(0, tiles - 2), tiles):
        leave(tile, tile & 1).wait()


def chunk(table, state, arrived, offsets, start, tiles, out):
    padded = pltpu.VMEM((FIELDS, EDGE + 6, SLOTS, LANES), F32)
    faces = FIELDS * 2 * 66 * tiles * SLOTS * LANES
    operands = (table, state, *arrived) + (() if out is None else (out,))
    return pl.pallas_call(
        functools.partial(chunk_kernel, start * LANES, tiles, offsets),
        in_specs=[SMEM] + [ANY] * (len(operands) - 1),
        out_specs=ANY,
        out_shape=jax.ShapeDtypeStruct(state.shape, F32),
        input_output_aliases={} if out is None else {5: 0},
        scratch_shapes=[
            pltpu.VMEM((tiles, SLOTS * FIELDS * EDGE, LANES), F32),
            pltpu.VMEM((2, FIELDS, SLOTS * EDGE, LANES), F32),
            padded,
            padded,
            pltpu.VMEM((EDGE + 6, SLOTS, LANES), F32),
            padded,
            pltpu.SemaphoreType.DMA((tiles,)),
            pltpu.SemaphoreType.DMA((2,)),
        ],
        cost_estimate=pl.CostEstimate(
            flops=faces * 90, bytes_accessed=tiles * FIELDS * 256 * LANES * 8, transcendentals=2 * faces
        ),
        compiler_params=params(),
        name="sections",
    )(*operands)


def edges_kernel(pieces, table, state, *refs):
    arrived, (first, last, head, tail, stage, sem) = refs[:-6], refs[-6:]
    for end, slot, low in ((0, 0, 0), (1, SLOTS - 1, 16)):
        code = table[slot]

        def load(source, f, columns, end=end):
            pltpu.make_async_copy(source, stage.at[end, f, :, columns], sem.at[end]).start()

        @pl.when(code < SLOTS)
        def _(code=code, low=low, load=load):
            row = pl.multiple_of(code * EDGE + low, 8)
            for f in range(FIELDS):
                load(state.at[f, pl.ds(row, 16), :], f, slice(None))

        for i, (peer, start, tiles) in enumerate(pieces):

            @pl.when((code >> 3) == peer + 1)
            def _(code=code, low=low, load=load, i=i, start=start, tiles=tiles):
                row = pl.multiple_of((code & 7) * FIELDS * EDGE + low, 8)
                for f in range(FIELDS):
                    load(arrived[i].at[pl.ds(row + f * EDGE, 16), :], f, pl.ds(start * LANES, tiles * LANES))

    copies = []
    for end, kept, sent in ((0, head, first), (1, tail, last)):
        pltpu.make_async_copy(stage.at[end], stage.at[end], sem.at[end]).wait()
        copies.append(pltpu.make_async_copy(stage.at[end, :, pl.ds(8 * end, 8), :], sent, sem.at[2 + end]))
        copies.append(pltpu.make_async_copy(stage.at[end], kept, sem.at[4 + end]))
        copies[-2].start()
        copies[-1].start()
    for copy in copies:
        copy.wait()


def edges(table, state, arrived, pieces):
    return pl.pallas_call(
        functools.partial(edges_kernel, pieces),
        in_specs=[SMEM] + [ANY] * (1 + len(arrived)),
        out_specs=[ANY] * 4,
        out_shape=[jax.ShapeDtypeStruct((FIELDS, rows, state.shape[2]), F32) for rows in (8, 8, 16, 16)],
        scratch_shapes=[pltpu.VMEM((2, FIELDS, 16, state.shape[2]), F32), pltpu.SemaphoreType.DMA((6,))],
        compiler_params=params(),
        name="edges",
    )(table, state, *arrived)


def border_kernel(before, after, head, tail, _, out, lines, result, us, gs, bs, s1, sem):
    for tile in range(TILES):
        columns = pl.ds(tile * LANES, LANES)
        for end, row, source, rows in ((0, 0, before, 8), (0, 8, head, 16), (1, 0, tail, 16), (1, 16, after, 8)):
            pltpu.make_async_copy(
                source.at[:, :, columns], lines.at[end, :, pl.ds(tile * 24 + row, rows), :], sem
            ).start()
    pltpu.make_async_copy(lines, lines, sem).wait()

    @pl.loop(0, 2)
    def _(end):
        @pl.loop(0, FIELDS)
        def _(f):
            for x in range(20):
                us[f, x] = lines[end, f, pl.ds(2 + x, TILES, stride=24), :]

        physics(20, us, gs, bs)

        @pl.loop(0, FIELDS)
        def _(f):
            def emit(k, u, change):
                s1[f, k] = u - STEP * change

            update(14, us, gs, bs, f, emit)

        physics(14, s1, gs, bs)

        @pl.loop(0, FIELDS)
        def _(f):
            def emit(k, u, change):
                result[end, f, pl.ds(k, TILES, stride=8), :] = 0.5 * us[f, 6 + k] + (0.5 * u - (0.5 * STEP) * change)

            update(8, s1, gs, bs, f, emit)

        for tile in range(TILES):
            pltpu.make_async_copy(
                result.at[end, :, pl.ds(tile * 8, 8), :],
                out.at[:, pl.ds(pl.multiple_of(end * 248, 8), 8), pl.ds(tile * LANES, LANES)],
                sem,
            ).start()

    pltpu.make_async_copy(result, result, sem).wait()


def border(before, after, head, tail, out):
    return pl.pallas_call(
        border_kernel,
        in_specs=[ANY] * 5,
        out_specs=ANY,
        out_shape=jax.ShapeDtypeStruct(out.shape, F32),
        input_output_aliases={4: 0},
        scratch_shapes=[
            pltpu.VMEM((2, FIELDS, TILES * 24, LANES), F32),
            pltpu.VMEM((2, FIELDS, TILES * 8, LANES), F32),
            pltpu.VMEM((FIELDS, 20, TILES, LANES), F32),
            pltpu.VMEM((FIELDS, 20, TILES, LANES), F32),
            pltpu.VMEM((20, TILES, LANES), F32),
            pltpu.VMEM((FIELDS, 14, TILES, LANES), F32),
            pltpu.SemaphoreType.DMA,
        ],
        compiler_params=params(),
        name="border",
    )(before, after, head, tail, out)


def ring(value, axis, step):
    count = lax.axis_size(axis)
    return lax.ppermute(value, axis, [(i, (i + step) % count) for i in range(count)])


def shards(state, target):
    pieces = [[(peer, sum(sizes[:i]), sizes[i]) for i in range(len(sizes))] for peer, sizes in enumerate(PIECES)]
    early = [pieces[peer][0] for peer in (2, 0, 1)]
    late = sorted((piece for group in pieces for piece in group[1:]), key=lambda piece: piece[1])
    order = early + late
    sent = list(pack(target, state, early, True)) + list(pack(target, state, late, False))
    arrived = {piece: ring(value, "col", OFFSETS[piece[0] + 1]) for piece, value in zip(order, sent, strict=True)}
    table = make_table(target, [arrived[pieces[peer][0]] for peer in range(3)])
    out, start = None, 0
    for tiles in CHUNKS:
        if start + tiles == TILES:
            ready, out = lax.optimization_barrier((table, out))
            first, last, head, tail = edges(ready, state, [arrived[piece] for piece in order], order)
            line = ("row", "col")
            before, after = ring(last, line, 1), ring(first, line, -1)
        used = [next(p for p in group if p[1] <= start < p[1] + p[2]) for group in pieces]
        offsets = [start - piece[1] for piece in used]
        out = chunk(table, state, [arrived[piece] for piece in used], offsets, start, tiles, out)
        start += tiles
    return border(before, after, head, tail, out)


def solution(mesh):
    return jax.shard_map(
        shards,
        mesh=mesh,
        in_specs=(P(None, ("row", "col"), None), P(("row", "col"))),
        out_specs=P(None, ("row", "col"), None),
        check_vma=False,
    )
```

```python
import collections
import functools

import jax
import jax.numpy as jnp
from jax import lax
from jax.experimental import pallas as pl
from jax.experimental.pallas import tpu as pltpu
from jax.sharding import PartitionSpec as P

FIELDS = 5
EDGE = 32
SLOTS = 8
LANES = 128
TILES = 8
CHUNKS = (1, 1, 3, 3)
BOTH, ONE, TWO = (0, 1), (0,), (1,)
Piece = collections.namedtuple("Piece", ("name", "peer", "ranks", "start", "tiles", "relay", "gates"))
PLAN = (
    Piece("a2", 2, BOTH, 0, 2, True, ()),
    Piece("a0", 0, BOTH, 0, 2, False, ()),
    Piece("a1", 1, BOTH, 0, 2, False, ()),
    Piece("b2", 2, BOTH, 2, 3, True, ("a0", "a1")),
    Piece("b0", 0, BOTH, 2, 6, False, ("a0", "a1", "a2'")),
    Piece("b1", 1, BOTH, 2, 6, False, ("a0", "a1", "a2'")),
    Piece("c2", 2, BOTH, 5, 3, False, ("b2", "out1")),
)
EARLY = 3
RELAY = tuple((col, (col + (4 if col & 1 else -4)) & 15) for col in range(16))
OFFSETS = (0, 1, -1, 8)
BOX_ROWS = FIELDS * EDGE
STEP = 0.05 / 6.0
TILE_COST = 6_000_000_000
PAD = 4
ANY = pl.BlockSpec(memory_space=pl.ANY)
HBM = pl.BlockSpec(memory_space=pltpu.HBM)
SMEM = pl.BlockSpec(memory_space=pltpu.SMEM)
F32 = jnp.float32


def params(mib=20):
    return pltpu.CompilerParams(vmem_limit_bytes=mib << 20)


def inverse(value):
    return pl.reciprocal(value, approx=True)


def side(t0, t1, t2, a01, a12):
    r0, r1, r2 = inverse(t0), inverse(t1), inverse(t2)
    p0, p1, p2 = (1.0 / 3.0) * (r0 * r0), r1 * r1, r2 * r2
    return (p0 * (a01 + a01) + p2 * a12) * inverse((p0 + p2) + (p1 + p1))


def rough(first):
    return (13.0 / 3.0 * first) * first + 0.75e-6


def square(value):
    return value * value


def face_value(au, ag, fu, fg, base, beta):
    bu = [beta * value for value in au]
    ap = [ag[i] + bu[i] for i in range(3)]
    am = [ag[i] - bu[i] for i in range(1, 4)]
    bf = [beta * value for value in fu]
    fp1, fp2 = fg[0] + bf[0], fg[1] + bf[1]
    fm1, fm2 = fg[2] - bf[2], fg[1] - bf[1]
    x1, x2 = rough(fp1), rough(fp2)
    plus = side(
        square(ap[0] + fp1) + x1, square(ap[1] + fp1) + x1, square(ap[2] - fp2) + x2, ap[0] - ap[1], ap[1] - ap[2]
    )
    x1, x2 = rough(fm1), rough(fm2)
    minus = side(
        square(am[2] - fm1) + x1, square(am[1] - fm1) + x1, square(am[0] + fm2) + x2, am[2] - am[1], am[1] - am[0]
    )
    return (base - (bu[1] - bu[2])) + (plus + minus)


def physics(count, us, gs, ss, emit):
    before = None
    for i in range(count):
        u = [us[f, i] for f in range(FIELDS)]
        r = inverse(u[0])
        half = 0.5 * u[1]
        half_velocity = half * r
        kinetic = (0.5 * r) * (u[1] * u[1] + u[2] * u[2] + u[3] * u[3])
        half_pressure = 0.2 * (u[4] - kinetic)
        g = (
            half,
            u[1] * half_velocity + half_pressure,
            u[2] * half_velocity,
            u[3] * half_velocity,
            (u[4] + (half_pressure + half_pressure)) * half_velocity,
        )
        for f in range(FIELDS):
            gs[f, i] = g[f]
            if before is not None:
                ss[0, f, i] = 0.375 * (u[f] - before[0][f])
                ss[1, f, i] = 0.375 * (g[f] - before[1][f])
        before = u, g
        sound = jnp.maximum((0.7 * half_pressure) * r, 1e-30)
        emit(i, jnp.abs(half_velocity) + sound * lax.rsqrt(sound))


def update(faces, us, gs, ss, bs, f, emit, wrap=None):
    first, last = faces
    u, g, fu, fg, au, ag, su, sg, base = ({} for _ in range(9))

    def cell(i):
        u[i], g[i] = us[f, i], gs[f, i]
        if i > first - 2:
            fu[i], fg[i] = u[i] - u[i - 1], g[i] - g[i - 1]
        if i >= first:
            su[i], sg[i] = ss[0, f, i], ss[1, f, i]
            au[i - 1], ag[i - 1] = fu[i] - fu[i - 1], fg[i] - fg[i - 1]
            base[i - 1] = 6.0 * g[i - 1] - ag[i - 1]

    for i in range(first - 2, first + 3):
        cell(i)
    previous = begin = None
    for i in range(first, last + 1):
        cell(i + 3)
        face = face_value(
            [au[j] for j in range(i - 1, i + 3)],
            [ag[j] for j in range(i - 1, i + 3)],
            [su[j] for j in range(i, i + 3)],
            [sg[j] for j in range(i, i + 3)],
            base[i] + base[i + 1],
            bs[i],
        )
        if previous is not None:
            emit(i, u[i], face - previous)
        else:
            begin = face
        previous = face
    if wrap is not None:
        emit(first, us[f, first], begin - wrap(previous))


def ghosts(ref, f):
    for k in range(1, 3):
        ref[f, k] = following(ref[f, EDGE + k])
    for k in range(3):
        ref[f, EDGE + 3 + k] = preceding(ref[f, 3 + k])


class Shifted:
    def __init__(self, ref, zero):
        self.ref, self.zero = ref, zero

    def __getitem__(self, i):
        return self.ref[i - self.zero]


def following(value):
    return pltpu.roll(value, 1, 0)


def preceding(value):
    return pltpu.roll(value, SLOTS - 1, 0)


def section(us, gs, ss, bs, emit):
    def speed(i, value):
        bs[i] = value

    inner = pl.ds(3, EDGE)
    physics(EDGE, us.at[:, inner], gs.at[:, inner], ss.at[:, :, inner], speed)
    first = bs[0]
    for i in range(EDGE):
        bs[i] = jnp.maximum(bs[i], bs[i + 1] if i + 1 < EDGE else preceding(first))

    @pl.loop(0, FIELDS)
    def _(f):
        ghosts(gs, f)
        for i in (3, EDGE + 3, EDGE + 4):
            ss[0, f, i] = 0.375 * (us[f, i] - us[f, i - 1])
            ss[1, f, i] = 0.375 * (gs[f, i] - gs[f, i - 1])
        update(
            (3, EDGE + 2),
            us,
            gs,
            ss,
            Shifted(bs, 3),
            f,
            lambda i, u, change: emit(f, i, u, change),
            following,
        )


def pack_kernel(pieces, first, target, state, *refs):
    count = len(pieces)
    outs, (stage, notes, in_sem, out_sem, note_sem) = refs[:count], refs[count:]
    col = lax.axis_index("col")
    steps = [((target[box] // SLOTS) - col) & 15 for box in range(SLOTS)]
    places, slots = [], []
    for peer in range(3):
        seen, place, slot = jnp.int32(0), [jnp.int32(0)] * 2, [jnp.int32(0)] * 2
        for box in range(SLOTS):
            hit = steps[box] == (OFFSETS[peer + 1] & 15)
            for rank in range(2):
                mine = hit & (seen == rank)
                place[rank] = jnp.where(mine, box, place[rank])
                slot[rank] = jnp.where(mine, target[box] & 7, slot[rank])
            seen = seen + hit.astype(jnp.int32)
        places.append(place)
        slots.append(slot)

    low = min(piece.start for piece in pieces) * LANES
    for i, piece in enumerate(pieces):
        for rank in piece.ranks:
            row = pl.multiple_of(places[piece.peer][rank] * EDGE, EDGE)
            for f in range(FIELDS):
                pltpu.make_async_copy(
                    state.at[f, pl.ds(row, EDGE), pl.ds(piece.start * LANES, piece.tiles * LANES)],
                    stage.at[
                        piece.peer,
                        pl.ds((rank * FIELDS + f) * EDGE, EDGE),
                        pl.ds(piece.start * LANES - low, piece.tiles * LANES),
                    ],
                    in_sem.at[i],
                ).start()

    def note(i):
        rows = len(pieces[i].ranks) * BOX_ROWS
        return pltpu.make_async_copy(notes.at[i], outs[i].at[pl.ds(rows, 8), pl.ds(0, LANES)], note_sem.at[i])

    if first:
        rows = lax.broadcasted_iota(jnp.int32, (8, LANES), 0)
        for i, piece in enumerate(pieces):
            mine = [slots[piece.peer][rank] for rank in piece.ranks]
            notes[i] = jnp.where(rows == 0, mine[0], mine[-1]).astype(F32)
            note(i).start()
    copies = []
    for i, piece in enumerate(pieces):
        rows = len(piece.ranks) * BOX_ROWS
        part = stage.at[
            piece.peer,
            pl.ds(piece.ranks[0] * BOX_ROWS, rows),
            pl.ds(piece.start * LANES - low, piece.tiles * LANES),
        ]
        pltpu.make_async_copy(part, part, in_sem.at[i]).wait()
        copies.append(pltpu.make_async_copy(part, outs[i].at[pl.ds(0, rows), :], out_sem.at[i]))
        copies[i].start()
    for i in range(count):
        copies[i].wait()
        if first:
            note(i).wait()


def pack(target, state, pieces, first):
    low = min(piece.start for piece in pieces)
    high = max(piece.start + piece.tiles for piece in pieces)
    return pl.pallas_call(
        functools.partial(pack_kernel, pieces, first),
        in_specs=[SMEM, HBM],
        out_specs=[ANY] * len(pieces),
        out_shape=[
            jax.ShapeDtypeStruct((len(piece.ranks) * BOX_ROWS + 8 * first, piece.tiles * LANES), F32)
            for piece in pieces
        ],
        scratch_shapes=[
            pltpu.VMEM((3, 2 * BOX_ROWS, (high - low) * LANES), F32),
            pltpu.VMEM((len(pieces), 8, LANES), F32),
            pltpu.SemaphoreType.DMA((len(pieces),)),
            pltpu.SemaphoreType.DMA((len(pieces),)),
            pltpu.SemaphoreType.DMA((len(pieces),)),
        ],
        compiler_params=params(56),
        name="pack",
    )(target, state)


def table_kernel(pieces, target, *refs):
    arrived, (table, notes, sem) = refs[:-3], refs[-3:]

    def note(i):
        rows = len(pieces[i].ranks) * BOX_ROWS
        return pltpu.make_async_copy(arrived[i].at[pl.ds(rows, 8), pl.ds(0, LANES)], notes.at[i], sem.at[i])

    for i in range(len(pieces)):
        note(i).start()
    col = lax.axis_index("col")
    for box in range(SLOTS):

        @pl.when(((target[box] // SLOTS) & 15) == col)
        def _(box=box):
            table[target[box] & 7] = box

    for i, piece in enumerate(pieces):
        note(i).wait()
        for place, rank in enumerate(piece.ranks):
            table[notes[i, place, 0].astype(jnp.int32) & 7] = 8 + 2 * piece.peer + rank


def make_table(target, pieces, arrived):
    return pl.pallas_call(
        functools.partial(table_kernel, pieces),
        in_specs=[SMEM] + [ANY] * len(arrived),
        out_specs=SMEM,
        out_shape=jax.ShapeDtypeStruct((SLOTS,), jnp.int32),
        scratch_shapes=[pltpu.SMEM((len(pieces), 8, LANES), F32), pltpu.SemaphoreType.DMA((len(pieces),))],
        compiler_params=params(),
        name="slots",
    )(target, *arrived)


def chunk_kernel(pieces, start, tiles, table, state, *refs):
    out, boxes, result, us, gs, ss, bs, s1, in_sem, out_sem = refs[-10:]

    pitch = BOX_ROWS + PAD
    for tile in range(tiles):
        for slot in range(SLOTS):
            code = table[slot]

            @pl.when(code < SLOTS)
            def _(tile=tile, slot=slot, code=code):
                for f in range(FIELDS):
                    pltpu.make_async_copy(
                        state.at[f, pl.ds(pl.multiple_of(code * EDGE, EDGE), EDGE), pl.ds((start + tile) * LANES, LANES)],
                        boxes.at[tile, pl.ds(slot * pitch + f * EDGE, EDGE), :],
                        in_sem.at[tile],
                    ).start()

            for i, piece in enumerate(pieces):
                for place, rank in enumerate(piece.ranks):

                    @pl.when(code == 8 + 2 * piece.peer + rank)
                    def _(tile=tile, slot=slot, i=i, place=place, column=(start - piece.start + tile) * LANES):
                        pltpu.make_async_copy(
                            refs[i].at[pl.ds(place * BOX_ROWS, BOX_ROWS), pl.ds(column, LANES)],
                            boxes.at[tile, pl.ds(slot * pitch, BOX_ROWS), :],
                            in_sem.at[tile],
                        ).start()

    def leave(tile, half):
        column = pl.multiple_of((start + tile) * LANES, LANES)
        return [
            pltpu.make_async_copy(
                result.at[half, :, pl.ds(slot * (EDGE + PAD), EDGE), :],
                out.at[:, pl.ds(slot * EDGE, EDGE), pl.ds(column, LANES)],
                out_sem.at[half],
            )
            for slot in range(SLOTS)
        ]

    def left(half):
        part = out.at[:, :, pl.ds(0, LANES)]
        pltpu.make_async_copy(part, part, out_sem.at[half]).wait()

    @pl.loop(0, tiles)
    def _(tile):
        half = tile & 1
        part = boxes.at[tile, pl.ds(0, SLOTS * BOX_ROWS), :]
        pltpu.make_async_copy(part, part, in_sem.at[tile]).wait()

        @pl.loop(0, FIELDS)
        def _(f):
            for x in range(EDGE):
                us[f, 3 + x] = boxes[tile, pl.ds(f * EDGE + x, SLOTS, stride=pitch), :]
            ghosts(us, f)

        def one(f, i, u, change):
            s1[f, i] = u - STEP * change

        section(us, gs, ss, bs, one)

        @pl.loop(0, FIELDS)
        def _(f):
            ghosts(s1, f)

        @pl.when(tile >= 2)
        def _():
            left(half)

        def two(f, i, u, change):
            value = 0.5 * ((us[f, i] + u) - STEP * change)
            result[half, f, pl.ds(i - 3, SLOTS, stride=EDGE + PAD), :] = value

        section(s1, gs, ss, bs, two)
        for copy in leave(tile, half):
            copy.start()

    for tile in range(max(0, tiles - 2), tiles):
        left(tile & 1)


def chunk(table, state, pieces, arrived, start, tiles, out):
    padded = pltpu.VMEM((FIELDS, EDGE + 6, SLOTS, LANES), F32)
    operands = (table, state, *arrived) + (() if out is None else (out,))
    return pl.pallas_call(
        functools.partial(chunk_kernel, pieces, start, tiles),
        in_specs=[SMEM, HBM] + [ANY] * len(arrived) + ([] if out is None else [HBM]),
        out_specs=HBM,
        out_shape=jax.ShapeDtypeStruct(state.shape, F32),
        input_output_aliases={} if out is None else {2 + len(arrived): 0},
        scratch_shapes=[
            pltpu.VMEM((tiles, SLOTS * (FIELDS * EDGE + PAD), LANES), F32),
            pltpu.VMEM((2, FIELDS, SLOTS * (EDGE + PAD), LANES), F32),
            padded,
            padded,
            pltpu.VMEM((2, FIELDS, EDGE + 6, SLOTS, LANES), F32),
            pltpu.VMEM((EDGE, SLOTS, LANES), F32),
            padded,
            pltpu.SemaphoreType.DMA((tiles,)),
            pltpu.SemaphoreType.DMA((2,)),
        ],
        cost_estimate=pl.CostEstimate(
            flops=tiles * TILE_COST, bytes_accessed=tiles * FIELDS * 256 * LANES * 8, transcendentals=0
        ),
        compiler_params=params(),
        name="sections",
    )(*operands)


def edges_kernel(pieces, table, state, *refs):
    arrived, (first, last, head, tail, stage, sem) = refs[:-6], refs[-6:]
    for end, slot, low in ((0, 0, 0), (1, SLOTS - 1, 16)):
        code = table[slot]

        def load(source, f, columns, end=end):
            pltpu.make_async_copy(source, stage.at[end, f, :, columns], sem.at[end]).start()

        @pl.when(code < SLOTS)
        def _(code=code, low=low, load=load):
            row = pl.multiple_of(code * EDGE + low, 8)
            for f in range(FIELDS):
                load(state.at[f, pl.ds(row, 16), :], f, slice(None))

        for i, piece in enumerate(pieces):
            for place, rank in enumerate(piece.ranks):

                @pl.when(code == 8 + 2 * piece.peer + rank)
                def _(low=low, load=load, i=i, piece=piece, place=place):
                    for f in range(FIELDS):
                        load(
                            arrived[i].at[pl.ds((place * FIELDS + f) * EDGE + low, 16), :],
                            f,
                            pl.ds(piece.start * LANES, piece.tiles * LANES),
                        )

    copies = []
    for end, kept, sent in ((0, head, first), (1, tail, last)):
        pltpu.make_async_copy(stage.at[end], stage.at[end], sem.at[end]).wait()
        copies.append(pltpu.make_async_copy(stage.at[end, :, pl.ds(8 * end, 8), :], sent, sem.at[2 + end]))
        copies.append(pltpu.make_async_copy(stage.at[end], kept, sem.at[4 + end]))
        copies[-2].start()
        copies[-1].start()
    for copy in copies:
        copy.wait()


def edges(table, state, arrived, pieces):
    return pl.pallas_call(
        functools.partial(edges_kernel, pieces),
        in_specs=[SMEM, HBM] + [ANY] * len(arrived),
        out_specs=[ANY] * 4,
        out_shape=[jax.ShapeDtypeStruct((FIELDS, rows, state.shape[2]), F32) for rows in (8, 8, 16, 16)],
        scratch_shapes=[pltpu.VMEM((2, FIELDS, 16, state.shape[2]), F32), pltpu.SemaphoreType.DMA((6,))],
        compiler_params=params(),
        name="edges",
    )(table, state, *arrived)


def border_kernel(end, near, far, old, out, lines, result, us, gs, ss, bs, s1, sem):
    pitch = 24 + PAD
    low, row = 2 + 2 * end, 248 * end
    for tile in range(TILES):
        columns = pl.ds(tile * LANES, LANES)
        for first, rows, source in ((0, 8, far), (8, 16, near)) if end == 0 else ((0, 16, near), (16, 8, far)):
            pltpu.make_async_copy(
                source.at[:, :, columns], lines.at[:, pl.ds(tile * pitch + first, rows), :], sem.at[0]
            ).start()
        pltpu.make_async_copy(
            old.at[:, pl.ds(row, 8), columns], result.at[:, pl.ds(tile * 12, 8), :], sem.at[1]
        ).start()

    def faces(speeds):
        def speed(i, value):
            if speeds:
                bs[i - 1] = jnp.maximum(speeds[-1], value)
            speeds.append(value)

        return speed

    part = lines.at[:, pl.ds(0, TILES * 24), :]
    pltpu.make_async_copy(part, part, sem.at[0]).wait()

    @pl.loop(0, FIELDS)
    def _(f):
        for x in range(18):
            us[f, x] = lines[f, pl.ds(low + x, TILES, stride=pitch), :]

    physics(18, us, gs, ss, faces([]))

    @pl.loop(0, FIELDS)
    def _(f):
        def one(i, u, change):
            s1[f, i - 3] = u - STEP * change

        update((2, 14), us, gs, ss, bs, f, one)

    physics(12, s1, gs, ss, faces([]))
    part = result.at[:, pl.ds(0, TILES * 8), :]
    pltpu.make_async_copy(part, part, sem.at[1]).wait()

    @pl.loop(0, FIELDS)
    def _(f):
        def two(i, u, change):
            value = 0.5 * ((us[f, i + 3] + u) - STEP * change)
            result[f, pl.ds(i - 3 + 2 * end, TILES, stride=12), :] = value

        update((2, 8), s1, gs, ss, bs, f, two)

    for tile in range(TILES):
        pltpu.make_async_copy(
            result.at[:, pl.ds(tile * 12, 8), :],
            out.at[:, pl.ds(row, 8), pl.ds(tile * LANES, LANES)],
            sem.at[2],
        ).start()
    pltpu.make_async_copy(part, part, sem.at[2]).wait()


def border(end, near, far, out):
    return pl.pallas_call(
        functools.partial(border_kernel, end),
        in_specs=[ANY] * 2 + [HBM],
        out_specs=HBM,
        out_shape=jax.ShapeDtypeStruct(out.shape, F32),
        input_output_aliases={2: 0},
        scratch_shapes=[
            pltpu.VMEM((FIELDS, TILES * 32, LANES), F32),
            pltpu.VMEM((FIELDS, TILES * 12, LANES), F32),
            pltpu.VMEM((FIELDS, 18, TILES, LANES), F32),
            pltpu.VMEM((FIELDS, 18, TILES, LANES), F32),
            pltpu.VMEM((2, FIELDS, 18, TILES, LANES), F32),
            pltpu.VMEM((18, TILES, LANES), F32),
            pltpu.VMEM((FIELDS, 12, TILES, LANES), F32),
            pltpu.SemaphoreType.DMA((3,)),
        ],
        compiler_params=params(),
        name="border",
    )(near, far, out)


def ring(value, axis, step):
    count = lax.axis_size(axis)
    return lax.ppermute(value, axis, [(i, (i + step) % count) for i in range(count)])


def shards(state, target):
    arrived, waiting = {}, []

    def prepare(pieces, gates):
        ready = target
        if gates:
            ready, _ = lax.optimization_barrier((target, [arrived[gate] for gate in gates]))
        waiting.extend(zip(pieces, pack(ready, state, pieces, not gates), strict=True))

    def start_ready():
        while waiting and all(gate in arrived for gate in waiting[0][0].gates):
            piece, value = waiting.pop(0)
            if piece.gates:
                value, _ = lax.optimization_barrier((value, [arrived[gate] for gate in piece.gates]))
            if piece.relay:
                arrived[piece.name + "'"] = lax.ppermute(value, "col", RELAY)
                arrived[piece.name] = lax.ppermute(arrived[piece.name + "'"], "col", RELAY)
            else:
                arrived[piece.name] = ring(value, "col", OFFSETS[piece.peer + 1])

    early = PLAN[:EARLY]
    prepare(early, ())
    start_ready()
    prepare(PLAN[EARLY:], ("a2'",))
    start_ready()
    table = make_table(target, early, [arrived[piece.name] for piece in early])
    out, start = None, 0
    for tiles in CHUNKS:
        if start + tiles == TILES:
            ready, out = lax.optimization_barrier((table, out))
            first, last, head, tail = edges(ready, state, [arrived[piece.name] for piece in PLAN], PLAN)
            line = ("row", "col")
            before, after = ring(last, line, 1), ring(first, line, -1)
        used = [piece for piece in PLAN if piece.start <= start < piece.start + piece.tiles]
        out = chunk(table, state, used, [arrived[piece.name] for piece in used], start, tiles, out)
        arrived[f"out{start}"] = out
        start += tiles
        start_ready()
    return border(1, tail, after, border(0, head, before, out))


def solution(mesh):
    return jax.shard_map(
        shards,
        mesh=mesh,
        in_specs=(P(None, ("row", "col"), None), P(("row", "col"))),
        out_specs=P(None, ("row", "col"), None),
        check_vma=False,
    )
```

```python
import collections
import functools

import jax
import jax.numpy as jnp
from jax import lax
from jax.experimental import pallas as pl
from jax.experimental.pallas import tpu as pltpu
from jax.sharding import PartitionSpec as P

FIELDS = 5
EDGE = 32
SLOTS = 8
LANES = 128
TILES = 8
CHUNKS = (1, 1, 3, 3)
BOTH, ONE, TWO = (0, 1), (0,), (1,)
Piece = collections.namedtuple("Piece", ("name", "peer", "ranks", "start", "tiles", "relay", "gates"))
PLAN = (
    Piece("a2", 2, BOTH, 0, 2, True, ()),
    Piece("a0", 0, BOTH, 0, 2, False, ()),
    Piece("a1", 1, BOTH, 0, 2, False, ()),
    Piece("b2", 2, BOTH, 2, 3, True, ("a0", "a1")),
    Piece("b0", 0, BOTH, 2, 6, False, ("a0", "a1", "a2'")),
    Piece("b1", 1, BOTH, 2, 6, False, ("a0", "a1", "a2'")),
    Piece("c2", 2, BOTH, 5, 3, False, ("b2", "out1")),
)
EARLY = 3
RELAY = tuple((col, (col + (4 if col & 1 else -4)) & 15) for col in range(16))
OFFSETS = (0, 1, -1, 8)
BOX_ROWS = FIELDS * EDGE
STEP = 0.05 / 6.0
TILE_COST = 6_000_000_000
PAD = 4
ANY = pl.BlockSpec(memory_space=pl.ANY)
HBM = pl.BlockSpec(memory_space=pltpu.HBM)
SMEM = pl.BlockSpec(memory_space=pltpu.SMEM)
F32 = jnp.float32


def params(mib=20):
    return pltpu.CompilerParams(vmem_limit_bytes=mib << 20)


def inverse(value):
    return pl.reciprocal(value, approx=True)


def side(t0, t1, t2, a01, a12):
    r0, r1, r2 = inverse(t0), inverse(t1), inverse(t2)
    p0, p1, p2 = (1.0 / 3.0) * (r0 * r0), r1 * r1, r2 * r2
    return (p0 * (a01 + a01) + p2 * a12) * inverse((p0 + p2) + (p1 + p1))


def rough(first):
    return (13.0 / 3.0 * first) * first + 0.75e-6


def square(value):
    return value * value


def face_value(au, ag, fu, fg, base, beta):
    bu = [beta * value for value in au]
    ap = [ag[i] + bu[i] for i in range(3)]
    am = [ag[i] - bu[i] for i in range(1, 4)]
    bf = [beta * value for value in fu]
    fp1, fp2 = fg[0] + bf[0], fg[1] + bf[1]
    fm1, fm2 = fg[2] - bf[2], fg[1] - bf[1]
    x1, x2 = rough(fp1), rough(fp2)
    plus = side(
        square(ap[0] + fp1) + x1, square(ap[1] + fp1) + x1, square(ap[2] - fp2) + x2, ap[0] - ap[1], ap[1] - ap[2]
    )
    x1, x2 = rough(fm1), rough(fm2)
    minus = side(
        square(am[2] - fm1) + x1, square(am[1] - fm1) + x1, square(am[0] + fm2) + x2, am[2] - am[1], am[1] - am[0]
    )
    return (base - (bu[1] - bu[2])) + (plus + minus)


def physics(count, us, gs, ss, emit):
    before = None
    for i in range(count):
        u = [us[f, i] for f in range(FIELDS)]
        r = inverse(u[0])
        half = 0.5 * u[1]
        half_velocity = half * r
        kinetic = (0.5 * r) * (u[1] * u[1] + u[2] * u[2] + u[3] * u[3])
        half_pressure = 0.2 * (u[4] - kinetic)
        g = (
            half,
            u[1] * half_velocity + half_pressure,
            u[2] * half_velocity,
            u[3] * half_velocity,
            (u[4] + (half_pressure + half_pressure)) * half_velocity,
        )
        for f in range(FIELDS):
            gs[f, i] = g[f]
            if before is not None:
                ss[0, f, i] = 0.375 * (u[f] - before[0][f])
                ss[1, f, i] = 0.375 * (g[f] - before[1][f])
        before = u, g
        sound = jnp.maximum((0.7 * half_pressure) * r, 1e-30)
        emit(i, jnp.abs(half_velocity) + sound * lax.rsqrt(sound))


def update(faces, us, gs, ss, bs, f, emit, wrap=None):
    first, last = faces
    u, g, fu, fg, au, ag, su, sg, base = ({} for _ in range(9))

    def cell(i):
        u[i], g[i] = us[f, i], gs[f, i]
        if i > first - 2:
            fu[i], fg[i] = u[i] - u[i - 1], g[i] - g[i - 1]
        if i >= first:
            su[i], sg[i] = ss[0, f, i], ss[1, f, i]
            au[i - 1], ag[i - 1] = fu[i] - fu[i - 1], fg[i] - fg[i - 1]
            base[i - 1] = 6.0 * g[i - 1] - ag[i - 1]

    for i in range(first - 2, first + 3):
        cell(i)
    previous = begin = None
    for i in range(first, last + 1):
        cell(i + 3)
        face = face_value(
            [au[j] for j in range(i - 1, i + 3)],
            [ag[j] for j in range(i - 1, i + 3)],
            [su[j] for j in range(i, i + 3)],
            [sg[j] for j in range(i, i + 3)],
            base[i] + base[i + 1],
            bs[i],
        )
        if previous is not None:
            emit(i, u[i], face - previous)
        else:
            begin = face
        previous = face
    if wrap is not None:
        emit(first, us[f, first], begin - wrap(previous))


def ghosts(ref, f):
    for k in range(1, 3):
        ref[f, k] = following(ref[f, EDGE + k])
    for k in range(3):
        ref[f, EDGE + 3 + k] = preceding(ref[f, 3 + k])


class Shifted:
    def __init__(self, ref, zero):
        self.ref, self.zero = ref, zero

    def __getitem__(self, i):
        return self.ref[i - self.zero]


def following(value):
    return pltpu.roll(value, 1, 0)


def preceding(value):
    return pltpu.roll(value, SLOTS - 1, 0)


def section(us, gs, ss, bs, emit):
    def speed(i, value):
        bs[i] = value

    inner = pl.ds(3, EDGE)
    physics(EDGE, us.at[:, inner], gs.at[:, inner], ss.at[:, :, inner], speed)
    first = bs[0]
    for i in range(EDGE):
        bs[i] = jnp.maximum(bs[i], bs[i + 1] if i + 1 < EDGE else preceding(first))

    @pl.loop(0, FIELDS)
    def _(f):
        ghosts(gs, f)
        for i in (3, EDGE + 3, EDGE + 4):
            ss[0, f, i] = 0.375 * (us[f, i] - us[f, i - 1])
            ss[1, f, i] = 0.375 * (gs[f, i] - gs[f, i - 1])
        update(
            (3, EDGE + 2),
            us,
            gs,
            ss,
            Shifted(bs, 3),
            f,
            lambda i, u, change: emit(f, i, u, change),
            following,
        )


def pack_kernel(pieces, first, target, state, *refs):
    count = len(pieces)
    outs, (stage, notes, in_sem, out_sem, note_sem) = refs[:count], refs[count:]
    col = lax.axis_index("col")
    steps = [((target[box] // SLOTS) - col) & 15 for box in range(SLOTS)]
    places, slots = [], []
    for peer in range(3):
        seen, place, slot = jnp.int32(0), [jnp.int32(0)] * 2, [jnp.int32(0)] * 2
        for box in range(SLOTS):
            hit = steps[box] == (OFFSETS[peer + 1] & 15)
            for rank in range(2):
                mine = hit & (seen == rank)
                place[rank] = jnp.where(mine, box, place[rank])
                slot[rank] = jnp.where(mine, target[box] & 7, slot[rank])
            seen = seen + hit.astype(jnp.int32)
        places.append(place)
        slots.append(slot)

    low = min(piece.start for piece in pieces) * LANES
    for i, piece in enumerate(pieces):
        for rank in piece.ranks:
            row = pl.multiple_of(places[piece.peer][rank] * EDGE, EDGE)
            for f in range(FIELDS):
                pltpu.make_async_copy(
                    state.at[f, pl.ds(row, EDGE), pl.ds(piece.start * LANES, piece.tiles * LANES)],
                    stage.at[
                        piece.peer,
                        pl.ds((rank * FIELDS + f) * EDGE, EDGE),
                        pl.ds(piece.start * LANES - low, piece.tiles * LANES),
                    ],
                    in_sem.at[i],
                ).start()

    def note(i):
        rows = len(pieces[i].ranks) * BOX_ROWS
        return pltpu.make_async_copy(notes.at[i], outs[i].at[pl.ds(rows, 8), pl.ds(0, LANES)], note_sem.at[i])

    if first:
        rows = lax.broadcasted_iota(jnp.int32, (8, LANES), 0)
        for i, piece in enumerate(pieces):
            mine = [slots[piece.peer][rank] for rank in piece.ranks]
            notes[i] = jnp.where(rows == 0, mine[0], mine[-1]).astype(F32)
            note(i).start()
    copies = []
    for i, piece in enumerate(pieces):
        rows = len(piece.ranks) * BOX_ROWS
        part = stage.at[
            piece.peer,
            pl.ds(piece.ranks[0] * BOX_ROWS, rows),
            pl.ds(piece.start * LANES - low, piece.tiles * LANES),
        ]
        pltpu.make_async_copy(part, part, in_sem.at[i]).wait()
        copies.append(pltpu.make_async_copy(part, outs[i].at[pl.ds(0, rows), :], out_sem.at[i]))
        copies[i].start()
    for i in range(count):
        copies[i].wait()
        if first:
            note(i).wait()


def pack(target, state, pieces, first):
    low = min(piece.start for piece in pieces)
    high = max(piece.start + piece.tiles for piece in pieces)
    return pl.pallas_call(
        functools.partial(pack_kernel, pieces, first),
        in_specs=[SMEM, HBM],
        out_specs=[ANY] * len(pieces),
        out_shape=[
            jax.ShapeDtypeStruct((len(piece.ranks) * BOX_ROWS + 8 * first, piece.tiles * LANES), F32)
            for piece in pieces
        ],
        scratch_shapes=[
            pltpu.VMEM((3, 2 * BOX_ROWS, (high - low) * LANES), F32),
            pltpu.VMEM((len(pieces), 8, LANES), F32),
            pltpu.SemaphoreType.DMA((len(pieces),)),
            pltpu.SemaphoreType.DMA((len(pieces),)),
            pltpu.SemaphoreType.DMA((len(pieces),)),
        ],
        compiler_params=params(56),
        name="pack",
    )(target, state)


def table_kernel(pieces, target, *refs):
    arrived, (table, notes, sem) = refs[:-3], refs[-3:]

    def note(i):
        rows = len(pieces[i].ranks) * BOX_ROWS
        return pltpu.make_async_copy(arrived[i].at[pl.ds(rows, 8), pl.ds(0, LANES)], notes.at[i], sem.at[i])

    for i in range(len(pieces)):
        note(i).start()
    col = lax.axis_index("col")
    seen, stay = jnp.int32(0), [jnp.int32(0)] * 4
    for box in range(SLOTS):
        hit = ((target[box] // SLOTS) & 15) == col
        for j in range(2):
            mine = hit & (seen == j)
            stay[j] = jnp.where(mine, box, stay[j])
            stay[2 + j] = jnp.where(mine, target[box] & 7, stay[2 + j])
        seen = seen + hit.astype(jnp.int32)
    for j in range(4):
        table[6 + j] = stay[j]
    for i, piece in enumerate(pieces):
        note(i).wait()
        for place, rank in enumerate(piece.ranks):
            table[2 * piece.peer + rank] = notes[i, place, 0].astype(jnp.int32) & 7


def make_table(target, pieces, arrived):
    return pl.pallas_call(
        functools.partial(table_kernel, pieces),
        in_specs=[SMEM] + [ANY] * len(arrived),
        out_specs=SMEM,
        out_shape=jax.ShapeDtypeStruct((10,), jnp.int32),
        scratch_shapes=[pltpu.SMEM((len(pieces), 8, LANES), F32), pltpu.SemaphoreType.DMA((len(pieces),))],
        compiler_params=params(),
        name="slots",
    )(target, *arrived)


def chunk_kernel(pieces, start, tiles, table, state, *refs):
    out, boxes, result, us, gs, ss, bs, s1, in_sem, out_sem = refs[-10:]

    pitch = BOX_ROWS + PAD
    for tile in range(tiles):
        for i, piece in enumerate(pieces):
            for place, rank in enumerate(piece.ranks):
                row = pl.multiple_of(table[2 * piece.peer + rank] * pitch, PAD)
                pltpu.make_async_copy(
                    refs[i].at[
                        pl.ds(place * BOX_ROWS, BOX_ROWS), pl.ds((start - piece.start + tile) * LANES, LANES)
                    ],
                    boxes.at[tile, pl.ds(row, BOX_ROWS), :],
                    in_sem.at[tile],
                ).start()
        for j in range(2):
            box = pl.multiple_of(table[6 + j] * EDGE, EDGE)
            row = pl.multiple_of(table[8 + j] * pitch, PAD)
            for f in range(FIELDS):
                pltpu.make_async_copy(
                    state.at[f, pl.ds(box, EDGE), pl.ds((start + tile) * LANES, LANES)],
                    boxes.at[tile, pl.ds(row + f * EDGE, EDGE), :],
                    in_sem.at[tile],
                ).start()

    def leave(tile, half):
        column = pl.multiple_of((start + tile) * LANES, LANES)
        return [
            pltpu.make_async_copy(
                result.at[half, :, pl.ds(slot * (EDGE + PAD), EDGE), :],
                out.at[:, pl.ds(slot * EDGE, EDGE), pl.ds(column, LANES)],
                out_sem.at[half],
            )
            for slot in range(SLOTS)
        ]

    def left(half):
        part = out.at[:, :, pl.ds(0, LANES)]
        pltpu.make_async_copy(part, part, out_sem.at[half]).wait()

    @pl.loop(0, tiles)
    def _(tile):
        half = tile & 1
        part = boxes.at[tile, pl.ds(0, SLOTS * BOX_ROWS), :]
        pltpu.make_async_copy(part, part, in_sem.at[tile]).wait()

        @pl.loop(0, FIELDS)
        def _(f):
            for x in range(EDGE):
                us[f, 3 + x] = boxes[tile, pl.ds(f * EDGE + x, SLOTS, stride=pitch), :]
            ghosts(us, f)

        def one(f, i, u, change):
            s1[f, i] = u - STEP * change

        section(us, gs, ss, bs, one)

        @pl.loop(0, FIELDS)
        def _(f):
            ghosts(s1, f)

        @pl.when(tile >= 2)
        def _():
            left(half)

        def two(f, i, u, change):
            value = 0.5 * ((us[f, i] + u) - STEP * change)
            result[half, f, pl.ds(i - 3, SLOTS, stride=EDGE + PAD), :] = value

        section(s1, gs, ss, bs, two)
        for copy in leave(tile, half):
            copy.start()

    for tile in range(max(0, tiles - 2), tiles):
        left(tile & 1)


def chunk(table, state, pieces, arrived, start, tiles, out):
    padded = pltpu.VMEM((FIELDS, EDGE + 6, SLOTS, LANES), F32)
    operands = (table, state, *arrived) + (() if out is None else (out,))
    return pl.pallas_call(
        functools.partial(chunk_kernel, pieces, start, tiles),
        in_specs=[SMEM, HBM] + [ANY] * len(arrived) + ([] if out is None else [HBM]),
        out_specs=HBM,
        out_shape=jax.ShapeDtypeStruct(state.shape, F32),
        input_output_aliases={} if out is None else {2 + len(arrived): 0},
        scratch_shapes=[
            pltpu.VMEM((tiles, SLOTS * (FIELDS * EDGE + PAD), LANES), F32),
            pltpu.VMEM((2, FIELDS, SLOTS * (EDGE + PAD), LANES), F32),
            padded,
            padded,
            pltpu.VMEM((2, FIELDS, EDGE + 6, SLOTS, LANES), F32),
            pltpu.VMEM((EDGE, SLOTS, LANES), F32),
            padded,
            pltpu.SemaphoreType.DMA((tiles,)),
            pltpu.SemaphoreType.DMA((2,)),
        ],
        cost_estimate=pl.CostEstimate(
            flops=tiles * TILE_COST, bytes_accessed=tiles * FIELDS * 256 * LANES * 8, transcendentals=0
        ),
        compiler_params=params(),
        name="sections",
    )(*operands)


def edges_kernel(pieces, table, state, *refs):
    arrived, (first, last, head, tail, stage, sem) = refs[:-6], refs[-6:]
    for end, slot, low in ((0, 0, 0), (1, SLOTS - 1, 16)):
        def load(source, f, columns, end=end):
            pltpu.make_async_copy(source, stage.at[end, f, :, columns], sem.at[end]).start()

        for j in range(2):

            @pl.when(table[8 + j] == slot)
            def _(j=j, low=low, load=load):
                row = pl.multiple_of(table[6 + j] * EDGE + low, 8)
                for f in range(FIELDS):
                    load(state.at[f, pl.ds(row, 16), :], f, slice(None))

        for i, piece in enumerate(pieces):
            for place, rank in enumerate(piece.ranks):

                @pl.when(table[2 * piece.peer + rank] == slot)
                def _(low=low, load=load, i=i, piece=piece, place=place):
                    for f in range(FIELDS):
                        load(
                            arrived[i].at[pl.ds((place * FIELDS + f) * EDGE + low, 16), :],
                            f,
                            pl.ds(piece.start * LANES, piece.tiles * LANES),
                        )

    copies = []
    for end, kept, sent in ((0, head, first), (1, tail, last)):
        pltpu.make_async_copy(stage.at[end], stage.at[end], sem.at[end]).wait()
        copies.append(pltpu.make_async_copy(stage.at[end, :, pl.ds(8 * end, 8), :], sent, sem.at[2 + end]))
        copies.append(pltpu.make_async_copy(stage.at[end], kept, sem.at[4 + end]))
        copies[-2].start()
        copies[-1].start()
    for copy in copies:
        copy.wait()


def edges(table, state, arrived, pieces):
    return pl.pallas_call(
        functools.partial(edges_kernel, pieces),
        in_specs=[SMEM, HBM] + [ANY] * len(arrived),
        out_specs=[ANY] * 4,
        out_shape=[jax.ShapeDtypeStruct((FIELDS, rows, state.shape[2]), F32) for rows in (8, 8, 16, 16)],
        scratch_shapes=[pltpu.VMEM((2, FIELDS, 16, state.shape[2]), F32), pltpu.SemaphoreType.DMA((6,))],
        compiler_params=params(),
        name="edges",
    )(table, state, *arrived)


def border_kernel(end, near, far, old, out, lines, result, us, gs, ss, bs, s1, sem):
    pitch = 24 + PAD
    low, row = 2 + 2 * end, 248 * end
    for tile in range(TILES):
        columns = pl.ds(tile * LANES, LANES)
        for first, rows, source in ((0, 8, far), (8, 16, near)) if end == 0 else ((0, 16, near), (16, 8, far)):
            pltpu.make_async_copy(
                source.at[:, :, columns], lines.at[:, pl.ds(tile * pitch + first, rows), :], sem.at[0]
            ).start()
        pltpu.make_async_copy(
            old.at[:, pl.ds(row, 8), columns], result.at[:, pl.ds(tile * 12, 8), :], sem.at[1]
        ).start()

    def faces(speeds):
        def speed(i, value):
            if speeds:
                bs[i - 1] = jnp.maximum(speeds[-1], value)
            speeds.append(value)

        return speed

    part = lines.at[:, pl.ds(0, TILES * 24), :]
    pltpu.make_async_copy(part, part, sem.at[0]).wait()

    @pl.loop(0, FIELDS)
    def _(f):
        for x in range(18):
            us[f, x] = lines[f, pl.ds(low + x, TILES, stride=pitch), :]

    physics(18, us, gs, ss, faces([]))

    @pl.loop(0, FIELDS)
    def _(f):
        def one(i, u, change):
            s1[f, i - 3] = u - STEP * change

        update((2, 14), us, gs, ss, bs, f, one)

    physics(12, s1, gs, ss, faces([]))
    part = result.at[:, pl.ds(0, TILES * 8), :]
    pltpu.make_async_copy(part, part, sem.at[1]).wait()

    @pl.loop(0, FIELDS)
    def _(f):
        def two(i, u, change):
            value = 0.5 * ((us[f, i + 3] + u) - STEP * change)
            result[f, pl.ds(i - 3 + 2 * end, TILES, stride=12), :] = value

        update((2, 8), s1, gs, ss, bs, f, two)

    for tile in range(TILES):
        pltpu.make_async_copy(
            result.at[:, pl.ds(tile * 12, 8), :],
            out.at[:, pl.ds(row, 8), pl.ds(tile * LANES, LANES)],
            sem.at[2],
        ).start()
    pltpu.make_async_copy(part, part, sem.at[2]).wait()


def border(end, near, far, out):
    return pl.pallas_call(
        functools.partial(border_kernel, end),
        in_specs=[ANY] * 2 + [HBM],
        out_specs=HBM,
        out_shape=jax.ShapeDtypeStruct(out.shape, F32),
        input_output_aliases={2: 0},
        scratch_shapes=[
            pltpu.VMEM((FIELDS, TILES * 32, LANES), F32),
            pltpu.VMEM((FIELDS, TILES * 12, LANES), F32),
            pltpu.VMEM((FIELDS, 18, TILES, LANES), F32),
            pltpu.VMEM((FIELDS, 18, TILES, LANES), F32),
            pltpu.VMEM((2, FIELDS, 18, TILES, LANES), F32),
            pltpu.VMEM((18, TILES, LANES), F32),
            pltpu.VMEM((FIELDS, 12, TILES, LANES), F32),
            pltpu.SemaphoreType.DMA((3,)),
        ],
        compiler_params=params(),
        name="border",
    )(near, far, out)


def ring(value, axis, step):
    count = lax.axis_size(axis)
    return lax.ppermute(value, axis, [(i, (i + step) % count) for i in range(count)])


def shards(state, target):
    arrived, waiting = {}, []

    def prepare(pieces, gates):
        ready = target
        if gates:
            ready, _ = lax.optimization_barrier((target, [arrived[gate] for gate in gates]))
        waiting.extend(zip(pieces, pack(ready, state, pieces, not gates), strict=True))

    def start_ready():
        while waiting and all(gate in arrived for gate in waiting[0][0].gates):
            piece, value = waiting.pop(0)
            if piece.gates:
                value, _ = lax.optimization_barrier((value, [arrived[gate] for gate in piece.gates]))
            if piece.relay:
                arrived[piece.name + "'"] = lax.ppermute(value, "col", RELAY)
                arrived[piece.name] = lax.ppermute(arrived[piece.name + "'"], "col", RELAY)
            else:
                arrived[piece.name] = ring(value, "col", OFFSETS[piece.peer + 1])

    early = PLAN[:EARLY]
    prepare(early, ())
    start_ready()
    prepare(PLAN[EARLY:], ("a2'",))
    start_ready()
    table = make_table(target, early, [arrived[piece.name] for piece in early])
    out, start = None, 0
    for tiles in CHUNKS:
        if start + tiles == TILES:
            ready, out = lax.optimization_barrier((table, out))
            first, last, head, tail = edges(ready, state, [arrived[piece.name] for piece in PLAN], PLAN)
            line = ("row", "col")
            before, after = ring(last, line, 1), ring(first, line, -1)
        used = [piece for piece in PLAN if piece.start <= start < piece.start + piece.tiles]
        out = chunk(table, state, used, [arrived[piece.name] for piece in used], start, tiles, out)
        arrived[f"out{start}"] = out
        start += tiles
        start_ready()
    return border(1, tail, after, border(0, head, before, out))


def solution(mesh):
    return jax.shard_map(
        shards,
        mesh=mesh,
        in_specs=(P(None, ("row", "col"), None), P(("row", "col"))),
        out_specs=P(None, ("row", "col"), None),
        check_vma=False,
    )
```
